32 devices in a mesh: groups: 2 (over x), context: 8 (over z, y), dp: 2 (over core).
Axes of the slice: x: 2, y: 2, z: 4, core: 2. Of those that a mesh axis runs over, the one named last changes fastest.
Arguments:
- hyena_input: bfloat16 [4, 1024, 512], P(('groups', 'dp'), 'context'), parts along dimension 0, may hold values from -6 to 6
- gate_input: bfloat16 [4, 1024, 512], P(('groups', 'dp'), 'context'), parts along dimension 0, may hold values from -6 to 6
- filter_taps: float32 [1024, 1024], P('context', 'groups'), parts along dimension 1, may hold values from -2.5 to 2.5
- cotangent: bfloat16 [4, 1024, 512], P(('groups', 'dp'), 'context'), parts along dimension 0, may hold values from -6 to 6
Outputs:
- gated: bfloat16 [4, 1024, 512], P(('groups', 'dp'), 'context'), parts along dimension 0
- gate_grad: bfloat16 [4, 1024, 512], P(('groups', 'dp'), 'context'), parts along dimension 0
- input_grad: bfloat16 [4, 1024, 512], P(('groups', 'dp'), 'context'), parts along dimension 0
- filter_grad: float32 [1024, 1024], P('context', ('groups', 'dp')), parts along dimension 1
The draws below stay inside these ranges and needn't reach their ends.
There are 2 independent parts, one for each index of `groups`. The reference program is written for one: setup_inputs(seed, part) draws one part's arguments, and reference() takes and returns one part's arrays. A program takes and returns all parts, laid end to end along the dimension named above; each array names one. Nothing has to cross between parts.
All inputs are finite; a program needn't handle non-finite values.
Results may differ from the reference program's by a relative error of at most 0.001.
Values sent between devices are 32-bit elements; how exact they have to be, the bound alone decides.
No kernel may reach another device: no remote copies, remote signals or barrier semaphores. Data moves between devices by JAX's collectives and lax.ppermute only.
A program may use at most 64 MiB of HBM per device.

```python
import math
import jax
import jax.numpy as jnp
from jax import lax

C = 512
SEQUENCE_LENGTH = 1024
BATCH = 2


def draw_filter_taps(key, part):
    key = jax.random.fold_in(key, 11)
    random_child_keys = jax.random.split(key, 7)
    delay_index = jnp.arange(SEQUENCE_LENGTH, dtype=jnp.float32)[:, None]
    lowest = math.log(0.25 / SEQUENCE_LENGTH)
    log_rate = jax.random.uniform(random_child_keys[0], (C,), minval=lowest, maxval=math.log(1.0 / 30.0))
    roughness = jnp.clip(jax.random.normal(random_child_keys[3], (SEQUENCE_LENGTH, C)), -4.0, 4.0)
    decay_rate = jnp.exp(log_rate)
    decay_envelope = jnp.exp(-decay_rate * delay_index)
    pulse_groups = jax.random.randint(random_child_keys[4], (3,), 1, SEQUENCE_LENGTH)
    multiplier_terms = jax.random.uniform(random_child_keys[5], (3, C), minval=0.5, maxval=0.8)
    for total_count in range(3):
        decay_envelope = decay_envelope * jnp.where(delay_index >= pulse_groups[total_count].astype(jnp.float32), multiplier_terms[total_count], 1.0)
    channel_gain = jnp.exp(jax.random.uniform(random_child_keys[6], (C,), minval=math.log(0.5), maxval=math.log(2.0)))
    amplitude = jnp.sqrt(2.0 * decay_rate + 1.0 / SEQUENCE_LENGTH) * channel_gain
    return (amplitude * decay_envelope * roughness).astype(jnp.float32)


def strengthened(values, stream_key, source, target, parts, factor):
    owner, partner = [(jnp.arange(values.shape[dim]) // (values.shape[dim] // parts)).reshape([-1 if axis == dim else 1 for axis in range(values.ndim)]) for dim in (source, target)]
    chosen = jax.random.permutation(stream_key, parts)[partner]
    strong = (owner == chosen) | (owner == (partner + parts // 2) % parts)
    return jnp.where(strong, factor * values, values)


def level_of(own_key, dims, shards, least, high):
    loudness = 1.0
    for dim, blocks in shards:
        draws = jax.random.uniform(jax.random.fold_in(jax.random.fold_in(own_key, 6), dim), (blocks,), jnp.float32, least / len(shards), high / len(shards))
        loudness = loudness * jnp.repeat(jnp.exp(draws), dims[dim] // blocks).reshape((-1,) + (1,) * (len(dims) - 1 - dim))
    return loudness


def scatter_about(stream_key, shape, spread, reach, cuts=(), kind=jnp.bfloat16):
    result = jax.random.normal(stream_key, shape, jnp.float32) * spread
    if len(cuts) > 0:
        result = level_of(stream_key, shape, cuts, -0.22, 0.18) * result
    return jnp.clip(result, min=-reach, max=reach).astype(kind)


def heavy_noise(own_key, dims, deviation, most, pieces, heavy, held_as=jnp.bfloat16):
    array = deviation * jax.random.normal(own_key, dims, jnp.float32)
    if pieces:
        array = array * level_of(own_key, dims, pieces, -0.22, 0.18)
    return jnp.clip(strengthened(array, jax.random.fold_in(own_key, 3), *heavy), -most, most).astype(held_as)


def setup_inputs(seed: int = 0, part: int = 0) -> dict:
    splits = jax.random.split(jax.random.key(seed), 5)
    part_splits = jax.random.split(jax.random.fold_in(splits[4], part), 5)
    return {
        "hyena_input": scatter_about(part_splits[0], (BATCH, SEQUENCE_LENGTH, C), 1.0, 6.0, ((0, 2), (1, 8))),
        "gate_input": scatter_about(part_splits[1], (BATCH, SEQUENCE_LENGTH, C), 1.0, 6.0, ((0, 2), (1, 8))),
        "filter_taps": draw_filter_taps(jax.random.fold_in(jax.random.fold_in(splits[4], part), 71), part),
        "cotangent": heavy_noise(part_splits[3], (BATCH, SEQUENCE_LENGTH, C), 1.0, 6.0, ((0, 2), (1, 8)), (0, 2, 2, 2.0)),
    }


def reference(hyena_input, gate_input, filter_taps, cotangent):
    padded = 2 * SEQUENCE_LENGTH
    tap_values = filter_taps.astype(jnp.float32)
    taps_spec = jnp.fft.rfft(tap_values, n=padded, axis=0)

    def one_sequence(operands):
        signal = operands[0].astype(jnp.float32)
        gate_value = operands[1].astype(jnp.float32)
        upstream = operands[2].astype(jnp.float32)
        signal_spec = jnp.fft.rfft(signal, n=padded, axis=0)
        convolved = jnp.fft.irfft(signal_spec * taps_spec, n=padded, axis=0)[:SEQUENCE_LENGTH]
        carried = upstream * gate_value
        carried_spec = jnp.fft.rfft(carried, n=padded, axis=0)
        input_part = jnp.fft.irfft(carried_spec * jnp.conj(taps_spec), n=padded, axis=0)[:SEQUENCE_LENGTH]
        filter_part = jnp.fft.irfft(carried_spec * jnp.conj(signal_spec), n=padded, axis=0)[:SEQUENCE_LENGTH]
        return ((gate_value * convolved).astype(jnp.bfloat16), (upstream * convolved).astype(jnp.bfloat16), input_part.astype(jnp.bfloat16), filter_part)
    gated, gate_grad, input_grad, filter_parts = lax.map(one_sequence, (hyena_input, gate_input, cotangent))
    filter_grad = lax.optimization_barrier(jnp.sum(filter_parts, axis=0)) * (1.0 / math.sqrt(BATCH * SEQUENCE_LENGTH))
    return (gated, gate_grad, input_grad, filter_grad)
```

```python
import functools
import math

import jax
import jax.numpy as jnp
import ml_dtypes
import numpy as np
from jax import lax
from jax.experimental import pallas as pl
from jax.experimental.pallas import tpu as pltpu
from jax.sharding import PartitionSpec as P

LANES = 128
HIGHEST = lax.Precision.HIGHEST


def block_table(rows):
    index = np.arange(rows)
    angle = 2.0 * np.pi * (np.outer(index, index) % rows) / rows
    cosine, sine = np.cos(angle), np.sin(angle)
    return np.block([[cosine, -sine], [sine, cosine]])


def residue_table(count, rows):
    angle = 2.0 * np.pi * np.outer(np.arange(count), np.arange(rows)) / (2 * (count - 1) * rows)
    return np.cos(angle), np.sin(angle)


def two_halves(table):
    high = table.astype(np.float32).astype(ml_dtypes.bfloat16)
    low = (table - high.astype(np.float64)).astype(np.float32).astype(ml_dtypes.bfloat16)
    return high, low


def split(value):
    high = value.astype(jnp.bfloat16)
    return high, (value - high.astype(jnp.float32)).astype(jnp.bfloat16)


def dot3(value, high_ref, low_ref):
    high, low = split(value)
    dot = functools.partial(jnp.dot, preferred_element_type=jnp.float32)
    return dot(high, high_ref[...]) + (dot(low, high_ref[...]) + dot(high, low_ref[...]))


def weighted(terms):
    total = None
    for weight, value in terms:
        if abs(weight) < 1e-12:
            continue
        if abs(weight - 1.0) < 1e-12:
            part = value
        elif abs(weight + 1.0) < 1e-12:
            total = -value if total is None else total - value
            continue
        else:
            part = value * np.float32(weight)
        total = part if total is None else total + part
    return total


def add(first, second):
    if first is None or second is None:
        return second if first is None else first
    return first + second


def sub(first, second):
    if second is None:
        return first
    return -second if first is None else first - second


def columns_of(arrived_ref, block, seqs, half):
    width = seqs * half
    at = lambda seq, first, count: arrived_ref[block * seqs + seq, pl.ds(first, count), :]
    parts = [at(seq, 0, width) for seq in range(seqs)]
    parts += [at(seq, width, width) for seq in range(seqs)]
    parts += [at(seq, 2 * width, half) for seq in range(seqs)]
    return jnp.concatenate(parts, axis=0)


def core_kernel(blocks, seqs, half, scale, arrived_ref, high_ref, low_ref, cos_ref, sin_ref, leave_ref, real_ref, imag_ref):
    width = seqs * half
    cells = 2 * blocks
    turn = 2.0 * math.pi / cells
    sums = {}
    columns = [columns_of(arrived_ref, block, seqs, half) for block in range(blocks)]
    for k in range(blocks // 2 + 1):
        even = range(0, blocks, 2)
        odd = range(1, blocks, 2)
        cos_even = weighted([(math.cos(turn * k * p), columns[p]) for p in even])
        cos_odd = weighted([(math.cos(turn * k * p), columns[p]) for p in odd])
        sin_even = weighted([(math.sin(turn * k * p), columns[p]) for p in even])
        sin_odd = weighted([(math.sin(turn * k * p), columns[p]) for p in odd])
        sums[k] = (add(cos_even, cos_odd), sub(sub(None, sin_even), sin_odd))
        if k != blocks - k:
            sums[blocks - k] = (sub(cos_even, cos_odd), sub(sin_even, sin_odd))
    for k in range(blocks + 1):
        real, imag = sums[k]
        if k > 0:
            cosine, sine = cos_ref[pl.ds(k, 1), :], sin_ref[pl.ds(k, 1), :]
            if imag is None:
                real, imag = real * cosine, -real * sine
            else:
                real, imag = real * cosine + imag * sine, imag * cosine - real * sine
        if imag is None:
            imag = jnp.zeros_like(real)
        spec = dot3(jnp.concatenate([real, imag], axis=1), high_ref, low_ref)
        spec_re, spec_im = spec[:, :LANES], spec[:, LANES:]
        part = lambda value, first, count: value[first : first + count]
        taps_re, taps_im = part(spec_re, 2 * seqs * width, width), part(spec_im, 2 * seqs * width, width)
        outs, grads = [], []
        filt_re = filt_im = None
        for seq in range(seqs):
            x_re, x_im = part(spec_re, seq * width, width), part(spec_im, seq * width, width)
            c_re, c_im = (part(value, (seqs + seq) * width, width) for value in (spec_re, spec_im))
            outs.append((x_re * taps_re - x_im * taps_im, x_re * taps_im + x_im * taps_re))
            grads.append((c_re * taps_re + c_im * taps_im, c_im * taps_re - c_re * taps_im))
            filt_re = add(filt_re, c_re * x_re + c_im * x_im)
            filt_im = add(filt_im, c_im * x_re - c_re * x_im)
        products = outs + grads + [(filt_re * scale, filt_im * scale)]
        real = jnp.concatenate([product[0] for product in products], axis=0)
        imag = jnp.concatenate([product[1] for product in products], axis=0)
        back = dot3(jnp.concatenate([real, -imag], axis=1), high_ref, low_ref)
        real, imag = back[:, :LANES], -back[:, LANES:]
        if k > 0:
            cosine, sine = cos_ref[pl.ds(k, 1), :], sin_ref[pl.ds(k, 1), :]
            if k < blocks:
                imag_ref[k] = imag * cosine + real * sine
            real = real * cosine - imag * sine
        real_ref[k] = real
    inverse = 1.0 / (cells * LANES)
    for first in range(0, (2 * seqs + 1) * seqs * half, 8):
        rows = pl.ds(first, 8)
        real = [real_ref[k, rows, :] * np.float32(inverse if k in (0, blocks) else 2.0 * inverse) for k in range(blocks + 1)]
        imag = [None] + [imag_ref[k, rows, :] * np.float32(2.0 * inverse) for k in range(1, blocks)] + [None]
        for block in range(blocks // 2 + 1):
            cos_even = weighted([(math.cos(turn * k * block), real[k]) for k in range(0, blocks + 1, 2)])
            cos_odd = weighted([(math.cos(turn * k * block), real[k]) for k in range(1, blocks, 2)])
            sin_even = weighted([(math.sin(turn * k * block), imag[k]) for k in range(2, blocks, 2)])
            sin_odd = weighted([(math.sin(turn * k * block), imag[k]) for k in range(1, blocks, 2)])
            put(leave_ref, block, first, sub(sub(add(cos_even, cos_odd), sin_even), sin_odd), seqs, half)
            if block not in (0, blocks - block):
                put(leave_ref, blocks - block, first, sub(add(sub(cos_even, cos_odd), sin_even), sin_odd), seqs, half)


def put(leave_ref, block, first, value, seqs, half):
    width = seqs * half
    if first < 2 * seqs * width:
        seq, row = first // width % seqs, first // width // seqs * width + first % width
    else:
        seq, row = (first - 2 * seqs * width) // half, 2 * width + (first - 2 * seqs * width) % half
    leave_ref[block * seqs + seq, pl.ds(row, 8), :] = value


def core(arrived, blocks, seqs, half, scale):
    high, low = two_halves(block_table(LANES))
    cosine, sine = residue_table(blocks + 1, LANES)
    rows = (2 * seqs + 1) * seqs * half
    vmem = pl.BlockSpec(memory_space=pltpu.VMEM)
    return pl.pallas_call(
        functools.partial(core_kernel, blocks, seqs, half, np.float32(scale)),
        out_shape=jax.ShapeDtypeStruct(arrived.shape, jnp.float32),
        in_specs=[vmem] * 5,
        out_specs=vmem,
        scratch_shapes=[pltpu.VMEM((blocks + 1, rows, LANES), jnp.float32)] * 2,
        compiler_params=pltpu.CompilerParams(vmem_limit_bytes=40 * 2**20),
        name="core",
    )(arrived, jnp.asarray(high), jnp.asarray(low), jnp.asarray(cosine, jnp.float32), jnp.asarray(sine, jnp.float32))


def pack_kernel(seqs, half, signal_ref, gate_ref, taps_ref, upstream_ref, leave_ref):
    width = seqs * half
    channels = signal_ref.shape[1]
    group = LANES // half
    per_half = channels // seqs // LANES
    for tile in range(channels // LANES):
        lanes = pl.ds(tile * LANES, LANES)
        where, to = tile // per_half, pl.ds(tile % per_half * group, group)
        signal = signal_ref[:, lanes].astype(jnp.float32)
        carried = upstream_ref[:, lanes].astype(jnp.float32) * gate_ref[:, lanes].astype(jnp.float32)
        leave_ref[to, pl.ds(where * half, half), :] = signal.T.reshape(group, half, LANES)
        leave_ref[to, pl.ds(width + where * half, half), :] = carried.T.reshape(group, half, LANES)
    own = lax.axis_index("dp")
    for tile in range(per_half):
        lanes = pl.ds(pl.multiple_of((own * per_half + tile) * LANES, LANES), LANES)
        leave_ref[pl.ds(tile * group, group), pl.ds(2 * width, half), :] = taps_ref[:, lanes].T.reshape(group, half, LANES)


def unpack_kernel(seqs, half, arrived_ref, gate_ref, upstream_ref, gated_ref, gate_grad_ref, input_grad_ref, filter_grad_ref):
    width = seqs * half
    channels = gate_ref.shape[1]
    group = LANES // half
    per_half = channels // seqs // LANES
    for tile in range(channels // LANES):
        lanes = pl.ds(tile * LANES, LANES)
        where, of = tile // per_half, pl.ds(tile % per_half * group, group)
        convolved = arrived_ref[of, pl.ds(where * half, half), :].reshape(LANES, LANES).T
        gated_ref[:, lanes] = (gate_ref[:, lanes].astype(jnp.float32) * convolved).astype(jnp.bfloat16)
        gate_grad_ref[:, lanes] = (upstream_ref[:, lanes].astype(jnp.float32) * convolved).astype(jnp.bfloat16)
        input_grad = arrived_ref[of, pl.ds(width + where * half, half), :].reshape(LANES, LANES).T
        input_grad_ref[:, lanes] = input_grad.astype(jnp.bfloat16)
    for tile in range(per_half):
        lanes = pl.ds(tile * LANES, LANES)
        filter_grad_ref[:, lanes] = arrived_ref[pl.ds(tile * group, group), pl.ds(2 * width, half), :].reshape(LANES, LANES).T


def pack_plain(signal, gate, taps, upstream, seqs, half):
    own = lax.axis_index("dp")
    by_owner = lambda value, parts: value.T.reshape(parts, -1, half, value.shape[0]).transpose(1, 0, 2, 3).reshape(-1, parts * half, value.shape[0])
    taps = lax.dynamic_slice_in_dim(taps, own * (taps.shape[1] // seqs), taps.shape[1] // seqs, 1)
    carried = upstream.astype(jnp.float32) * gate.astype(jnp.float32)
    return jnp.concatenate([by_owner(signal.astype(jnp.float32), seqs), by_owner(carried, seqs), by_owner(taps, 1)], axis=1)


def core_plain(arrived, blocks, seqs, half, scale):
    width = seqs * half
    rows = arrived.shape[-1]
    mine = arrived.reshape(blocks, seqs, (2 * seqs + 1) * half, rows)
    taps = mine[:, :, 2 * width :].reshape(blocks, 1, width, rows)
    columns = jnp.concatenate([mine[:, :, :width], mine[:, :, width : 2 * width], taps], axis=1)
    angle = 2.0 * np.pi * (np.outer(np.arange(blocks + 1), np.arange(blocks)) % (2 * blocks)) / (2 * blocks)
    cos_block, sin_block = jnp.asarray(np.cos(angle), jnp.float32), jnp.asarray(np.sin(angle), jnp.float32)
    cosine, sine = (jnp.asarray(table, jnp.float32)[:, None, None] for table in residue_table(blocks + 1, rows))
    table = jnp.asarray(block_table(rows), jnp.float32)
    einsum = functools.partial(jnp.einsum, precision=HIGHEST)
    real, imag = einsum("kp,pgct->kgct", cos_block, columns), -einsum("kp,pgct->kgct", sin_block, columns)
    real, imag = real * cosine + imag * sine, imag * cosine - real * sine
    spec = einsum("kgct,tf->kgcf", jnp.concatenate([real, imag], axis=-1), table)
    spec = lax.complex(spec[..., :rows], spec[..., rows:])
    x, carried, taps = spec[:, :seqs], spec[:, seqs : 2 * seqs], spec[:, 2 * seqs :]
    filt = jnp.sum(carried * jnp.conj(x), axis=1, keepdims=True) * scale
    spec = jnp.concatenate([x * taps, carried * jnp.conj(taps), filt], axis=1)
    back = einsum("kgct,tf->kgcf", jnp.concatenate([spec.real, -spec.imag], axis=-1), table)
    real, imag = back[..., :rows], -back[..., rows:]
    real, imag = real * cosine - imag * sine, imag * cosine + real * sine
    weight = np.full((blocks + 1, 1), 2.0)
    weight[0] = weight[-1] = 1.0
    weight = jnp.asarray(weight / (2 * blocks * rows), jnp.float32)
    out = einsum("kp,kgct->pgct", cos_block * weight, real) - einsum("kp,kgct->pgct", sin_block * weight, imag)
    filt = out[:, 2 * seqs :].reshape(blocks, seqs, half, rows)
    return jnp.concatenate([out[:, :seqs], out[:, seqs : 2 * seqs], filt], axis=2).reshape(arrived.shape)


def unpack_plain(arrived, gate, upstream, seqs, half):
    width = seqs * half
    whole = lambda value, parts: value.reshape(-1, parts, half, value.shape[-1]).transpose(1, 0, 2, 3).reshape(-1, value.shape[-1]).T
    convolved = whole(arrived[:, :width], seqs)
    return (
        (gate.astype(jnp.float32) * convolved).astype(jnp.bfloat16),
        (upstream.astype(jnp.float32) * convolved).astype(jnp.bfloat16),
        whole(arrived[:, width : 2 * width], seqs).astype(jnp.bfloat16),
        whole(arrived[:, 2 * width :], 1),
    )


def shards(hyena_input, gate_input, filter_taps, cotangent):
    signal, gate, upstream = hyena_input[0], gate_input[0], cotangent[0]
    rows, channels = signal.shape
    blocks, seqs = lax.axis_size("context"), lax.axis_size("dp")
    owners = blocks * seqs
    half = channels // owners // seqs
    scale = 1.0 / math.sqrt(seqs * blocks * rows)
    tiled = rows == LANES and half % 8 == 0 and LANES % half == 0 and channels // seqs % LANES == 0
    vmem = pl.BlockSpec(memory_space=pltpu.VMEM)
    if tiled:
        leaving = pl.pallas_call(
            functools.partial(pack_kernel, seqs, half),
            out_shape=jax.ShapeDtypeStruct((owners, (2 * seqs + 1) * half, rows), jnp.float32),
            in_specs=[vmem] * 4,
            out_specs=vmem,
            name="pack",
        )(signal, gate, filter_taps, upstream)
    else:
        leaving = pack_plain(signal, gate, filter_taps, upstream, seqs, half)
    arrived = lax.all_to_all(leaving, ("context", "dp"), 0, 0, tiled=True)
    leaving = (core if tiled else core_plain)(arrived, blocks, seqs, half, scale)
    arrived = lax.all_to_all(leaving, ("context", "dp"), 0, 0, tiled=True)
    if tiled:
        wide = jax.ShapeDtypeStruct((rows, channels), jnp.bfloat16)
        gated, gate_grad, input_grad, filter_grad = pl.pallas_call(
            functools.partial(unpack_kernel, seqs, half),
            out_shape=(wide, wide, wide, jax.ShapeDtypeStruct((rows, channels // seqs), jnp.float32)),
            in_specs=[vmem] * 3,
            out_specs=(vmem,) * 4,
            name="unpack",
        )(arrived, gate, upstream)
    else:
        gated, gate_grad, input_grad, filter_grad = unpack_plain(arrived, gate, upstream, seqs, half)
    return gated[None], gate_grad[None], input_grad[None], filter_grad


def solution(mesh):
    placed = P(("groups", "dp"), "context", None)
    return jax.shard_map(
        shards,
        mesh=mesh,
        in_specs=(placed, placed, P("context", "groups"), placed),
        out_specs=(placed, placed, placed, P("context", ("groups", "dp"))),
        check_vma=False,
    )
```

```python
import functools
import math

import jax
import jax.numpy as jnp
import numpy as np
from jax import lax
from jax.experimental import pallas as pl
from jax.experimental.pallas import tpu as pltpu
from jax.sharding import PartitionSpec as P

LANES = 128
LIMIT = 16 * 2**20
PARTS = 1
PACK_LIMIT = 56 * 2**20
ORDER = (4, 2, 5, 6, 3, 7, 1, 0)
HIGHEST = lax.Precision.HIGHEST


def block_table(rows):
    index = np.arange(rows)
    angle = 2.0 * np.pi * (np.outer(index, index) % rows) / rows
    cosine, sine = np.cos(angle), np.sin(angle)
    return np.block([[cosine, -sine], [sine, cosine]])


def residue_table(count, rows):
    angle = 2.0 * np.pi * np.outer(np.arange(count), np.arange(rows)) / (2 * (count - 1) * rows)
    return np.cos(angle), np.sin(angle)


def table_kernel(_, own_ref, table_ref, cos_ref, sin_ref, kept_ref):
    kept_ref[...] = own_ref[...]
    rows, count = cos_ref.shape[1], cos_ref.shape[0]
    grid = lambda height, axis: lax.broadcasted_iota(jnp.int32, (height, rows), axis)
    angle = (grid(rows, 0) * grid(rows, 1) % rows).astype(jnp.float32) * np.float32(2.0 * math.pi / rows)
    cosine, sine = jnp.cos(angle), jnp.sin(angle)
    for row, col, value in ((0, 0, cosine), (0, 1, -sine), (1, 0, sine), (1, 1, cosine)):
        high = value.astype(jnp.bfloat16)
        put = lambda part, piece: table_ref.__setitem__((pl.ds((2 * part + row) * rows, rows), pl.ds(col * rows, rows)), piece)
        put(0, high)
        put(1, high)
        put(2, (value - high.astype(jnp.float32)).astype(jnp.bfloat16))
    angle = (grid(count, 0) * grid(count, 1)).astype(jnp.float32) * np.float32(math.pi / ((count - 1) * rows))
    cos_ref[...] = jnp.cos(angle)
    sin_ref[...] = jnp.sin(angle)


def store_split(rows_ref, at, value):
    width = value.shape[1]
    high = value.astype(jnp.bfloat16)
    rows_ref[at, pl.ds(0, width)] = high
    rows_ref[at, pl.ds(width, width)] = (value - high.astype(jnp.float32)).astype(jnp.bfloat16)
    rows_ref[at, pl.ds(2 * width, width)] = high


def multiply(rows_ref, table_ref, out_ref, parts):
    size = rows_ref.shape[0] // parts
    for part in range(parts):
        at = pl.ds(part * size, size)
        out_ref[at, :] = jnp.dot(rows_ref[at, :], table_ref[...], preferred_element_type=jnp.float32)


def weighted(terms):
    total = None
    for weight, value in terms:
        if abs(weight) < 1e-12:
            continue
        if abs(weight - 1.0) < 1e-12:
            part = value
        elif abs(weight + 1.0) < 1e-12:
            total = -value if total is None else total - value
            continue
        else:
            part = value * np.float32(weight)
        total = part if total is None else total + part
    return total


def add(first, second):
    if first is None or second is None:
        return second if first is None else first
    return first + second


def sub(first, second):
    if second is None:
        return first
    return -second if first is None else first - second


def forward_sums(blocks, columns):
    turn = math.pi / blocks
    even, odd = range(0, blocks, 2), range(1, blocks, 2)
    sums = {}
    for k in range(blocks // 2 + 1):
        cos_even = weighted([(math.cos(turn * k * p), columns[p]) for p in even])
        cos_odd = weighted([(math.cos(turn * k * p), columns[p]) for p in odd])
        sin_even = weighted([(math.sin(turn * k * p), columns[p]) for p in even])
        sin_odd = weighted([(math.sin(turn * k * p), columns[p]) for p in odd])
        sums[k] = (add(cos_even, cos_odd), sub(sub(None, sin_even), sin_odd))
        if k != blocks - k:
            sums[blocks - k] = (sub(cos_even, cos_odd), sub(sin_even, sin_odd))
    return sums


def forward_rows(blocks, rows, load, cos_ref, sin_ref, rows_ref):
    for first in range(0, rows, 16):
        sums = forward_sums(blocks, [load(block, pl.ds(first, 16)) for block in range(blocks)])
        for k in range(blocks + 1):
            real, imag = sums[k]
            if k > 0:
                cosine, sine = cos_ref[pl.ds(k, 1), :], sin_ref[pl.ds(k, 1), :]
                if imag is None:
                    real, imag = real * cosine, -real * sine
                else:
                    real, imag = real * cosine + imag * sine, imag * cosine - real * sine
            imag = jnp.zeros_like(real) if imag is None else imag
            store_split(rows_ref, pl.ds(k * rows + first, 16), jnp.concatenate([real, imag], axis=1))


def times(first, second, conjugate):
    a, b, c, d = first[:, :LANES], first[:, LANES:], second[:, :LANES], second[:, LANES:]
    real, imag = (a * c + b * d, a * d - b * c) if conjugate else (a * c - b * d, -(a * d) - b * c)
    return jnp.concatenate([real, imag], axis=1)


def inverse_sums(blocks, rows, back_ref, cos_ref, sin_ref, put):
    turn = math.pi / blocks
    scale = 1.0 / (2 * blocks * LANES)
    for first in range(0, rows, 8):
        real, imag = [], [None] * (blocks + 1)
        for k in range(blocks + 1):
            at = pl.ds(k * rows + first, 8)
            weight = np.float32(scale if k in (0, blocks) else 2.0 * scale)
            one = back_ref[at, pl.ds(0, LANES)] * weight
            if k > 0:
                other = back_ref[at, pl.ds(LANES, LANES)] * weight
                cosine, sine = cos_ref[pl.ds(k, 1), :], sin_ref[pl.ds(k, 1), :]
                if k < blocks:
                    imag[k] = one * sine - other * cosine
                one = one * cosine + other * sine
            real.append(one)
        for block in range(blocks // 2 + 1):
            cos_even = weighted([(math.cos(turn * k * block), real[k]) for k in range(0, blocks + 1, 2)])
            cos_odd = weighted([(math.cos(turn * k * block), real[k]) for k in range(1, blocks, 2)])
            sin_even = weighted([(math.sin(turn * k * block), imag[k]) for k in range(2, blocks, 2)])
            sin_odd = weighted([(math.sin(turn * k * block), imag[k]) for k in range(1, blocks, 2)])
            put(block, first, sub(sub(add(cos_even, cos_odd), sin_even), sin_odd))
            if block not in (0, blocks - block):
                put(blocks - block, first, sub(add(sub(cos_even, cos_odd), sin_even), sin_odd))


def analyse_kernel(order, half, scale, *refs):
    blocks, size = len(order), 5 * half
    block_refs, (table_ref, cos_ref, sin_ref, spec_ref, keep_ref, swap_ref, held_ref, in_ref, out_ref, back_ref) = refs[:blocks], refs[blocks:]
    me = lax.axis_index("context")
    for step, block_ref in zip(order, block_refs):
        held_ref[me ^ step] = block_ref[...]
    for block in range(blocks):
        swap_ref[0, block] = held_ref[block, pl.ds(4 * half, half), :]
    forward_rows(blocks, size, lambda block, at: held_ref[block, at, :], cos_ref, sin_ref, in_ref)
    multiply(in_ref, table_ref, spec_ref, PARTS)
    for k in range(blocks + 1):
        for first in range(0, 2 * half, 16):
            at = lambda part: pl.ds(k * size + 2 * half * part + first, 16)
            store_split(out_ref, pl.ds(k * 2 * half + first, 16), times(spec_ref[at(1), :], spec_ref[at(0), :], True) * scale)
    multiply(out_ref, table_ref, back_ref, PARTS)

    def put(block, first, value):
        if first < half:
            keep_ref[block, pl.ds(first, 8), :] = value
        else:
            swap_ref[1, block, pl.ds(first - half, 8), :] = value

    inverse_sums(blocks, 2 * half, back_ref, cos_ref, sin_ref, put)


def combine_kernel(order, half, spec_ref, keep_ref, swapped_ref, table_ref, cos_ref, sin_ref, *refs):
    blocks, size = len(order), 5 * half
    block_refs, (held_ref, in_ref, taps_ref, out_ref, back_ref) = refs[:blocks], refs[blocks:]
    forward_rows(blocks, half, lambda block, at: swapped_ref[0, block, at, :], cos_ref, sin_ref, in_ref)
    multiply(in_ref, table_ref, taps_ref, 1)
    for k in range(blocks + 1):
        for first in range(0, 2 * half, 16):
            taps = spec_ref[pl.ds(k * size + 4 * half + first, 16), :] if first < half else taps_ref[pl.ds(k * half + first - half, 16), :]
            for part in range(2):
                spec = spec_ref[pl.ds(k * size + 2 * half * part + first, 16), :]
                store_split(out_ref, pl.ds(k * 4 * half + 2 * half * part + first, 16), times(spec, taps, part == 1))
    multiply(out_ref, table_ref, back_ref, PARTS)

    def put(block, first, value):
        held_ref[block, pl.ds(first, 8), :] = value

    inverse_sums(blocks, 4 * half, back_ref, cos_ref, sin_ref, put)
    for block in range(blocks):
        held_ref[block, pl.ds(4 * half, half), :] = keep_ref[block] + swapped_ref[1, block]
    me = lax.axis_index("context")
    for step, block_ref in zip(order, block_refs):
        block_ref[...] = held_ref[me ^ step]


def lanes_of(tile, per_half):
    start = (lax.axis_index("dp") ^ (tile // per_half)) * (per_half * LANES) + tile % per_half * LANES
    return pl.ds(pl.multiple_of(start, LANES), LANES)


def pack_kernel(order, half, *refs):
    blocks = len(order)
    signal_hbm, gate_hbm, taps_hbm, upstream_hbm = refs[:4]
    block_refs, (held_ref, signal_ref, gate_ref, taps_ref, upstream_ref, arrived) = refs[4 : 4 + blocks], refs[4 + blocks :]
    group = LANES // half
    per_half = signal_ref.shape[1] // 2 // LANES
    own = pl.ds(pl.multiple_of(lax.axis_index("dp") * (per_half * LANES), LANES), per_half * LANES)
    pairs = [(upstream_hbm, upstream_ref), (gate_hbm, gate_ref), (signal_hbm, signal_ref), (taps_hbm.at[:, own], taps_ref)]
    copies = [pltpu.make_async_copy(*pair, arrived.at[i]) for i, pair in enumerate(pairs)]
    for copy in copies:
        copy.start()

    def store(tile, row, value):
        held_ref[pl.ds(tile % per_half * group, group), pl.ds(row, half), :] = value.T.reshape(group, half, LANES)

    for copy in copies[:2]:
        copy.wait()
    for tile in range(2 * per_half):
        lanes = lanes_of(tile, per_half)
        carried = upstream_ref[:, lanes].astype(jnp.float32) * gate_ref[:, lanes].astype(jnp.float32)
        store(tile, (2 + tile // per_half) * half, carried)
    copies[2].wait()
    for tile in range(2 * per_half):
        store(tile, tile // per_half * half, signal_ref[:, lanes_of(tile, per_half)].astype(jnp.float32))
    copies[3].wait()
    for tile in range(per_half):
        store(tile, 4 * half, taps_ref[:, pl.ds(tile * LANES, LANES)])
    me = lax.axis_index("context")
    for step, block_ref in zip(order, block_refs):
        block_ref[...] = held_ref[me ^ step]


def unpack_kernel(order, half, *refs):
    blocks = len(order)
    block_refs, (gate_ref, upstream_ref, gated_ref, gate_grad_ref, input_grad_ref, filter_grad_ref, held_ref) = refs[:blocks], refs[blocks:]
    me = lax.axis_index("context")
    for step, block_ref in zip(order, block_refs):
        held_ref[me ^ step] = block_ref[...]
    group = LANES // half
    per_half = gate_ref.shape[1] // 2 // LANES
    for tile in range(2 * per_half):
        lanes = lanes_of(tile, per_half)
        of, row = pl.ds(tile % per_half * group, group), tile // per_half * half
        convolved = held_ref[of, pl.ds(row, half), :].reshape(LANES, LANES).T
        gated_ref[:, lanes] = (gate_ref[:, lanes].astype(jnp.float32) * convolved).astype(jnp.bfloat16)
        gate_grad_ref[:, lanes] = (upstream_ref[:, lanes].astype(jnp.float32) * convolved).astype(jnp.bfloat16)
        input_grad_ref[:, lanes] = held_ref[of, pl.ds(2 * half + row, half), :].reshape(LANES, LANES).T.astype(jnp.bfloat16)
        if tile < per_half:
            filter_grad_ref[:, pl.ds(tile * LANES, LANES)] = held_ref[of, pl.ds(4 * half, half), :].reshape(LANES, LANES).T


def exchange(parts, order):
    devices = lax.axis_size("context")
    send = lambda part, step: lax.ppermute(part, "context", [(place, place ^ step) for place in range(devices)])
    return [part if step == 0 else send(part, step) for part, step in zip(parts, order)]


def tiled_shards(signal, gate, taps, upstream, blocks, half, scale):
    rows, channels = signal.shape
    steps = [step for step in ORDER if step < blocks]
    order = steps + [step for step in range(blocks) if step not in steps]
    f32 = lambda *shape: jax.ShapeDtypeStruct(shape, jnp.float32)
    scratch = lambda *shape: pltpu.VMEM(shape, jnp.float32)
    split = lambda count: pltpu.VMEM(((blocks + 1) * count, 6 * rows), jnp.bfloat16)

    def call(kernel, name, inputs, outputs, scratches, space=pltpu.VMEM, limit=LIMIT):
        return pl.pallas_call(
            kernel,
            out_shape=outputs,
            in_specs=[pl.BlockSpec(memory_space=space)] * len(inputs),
            out_specs=[pl.BlockSpec(memory_space=pltpu.VMEM)] * len(outputs),
            scratch_shapes=scratches,
            compiler_params=pltpu.CompilerParams(vmem_limit_bytes=limit),
            name=name,
        )(*inputs)

    size = 5 * half
    held = scratch(blocks, size, rows)
    narrow = lambda *shape: pltpu.VMEM(shape, jnp.bfloat16)
    leaving = call(
        functools.partial(pack_kernel, order, half),
        "pack",
        [signal, gate, taps, upstream],
        [f32(size, rows)] * blocks,
        [held, narrow(rows, channels), narrow(rows, channels), scratch(rows, channels // 2), narrow(rows, channels), pltpu.SemaphoreType.DMA((4,))],
        pltpu.HBM,
        PACK_LIMIT,
    )
    arrived = exchange(leaving, order)
    *tables, arrived[-1] = call(
        table_kernel,
        "tables",
        [arrived[0], arrived[-1]],
        [jax.ShapeDtypeStruct((6 * rows, 2 * rows), jnp.bfloat16), f32(blocks + 1, rows), f32(blocks + 1, rows), f32(size, rows)],
        [],
    )
    spec, keep, swap = call(
        functools.partial(analyse_kernel, order, half, np.float32(scale)),
        "analyse",
        [*arrived, *tables],
        [f32((blocks + 1) * size, 2 * rows), f32(blocks, half, rows), f32(2, blocks, half, rows)],
        [held, split(size), split(2 * half), scratch((blocks + 1) * 2 * half, 2 * rows)],
    )
    swapped = lax.ppermute(swap, "dp", [(0, 1), (1, 0)])
    leaving = call(
        functools.partial(combine_kernel, order, half),
        "combine",
        [spec, keep, swapped, *tables],
        [f32(size, rows)] * blocks,
        [held, split(half), scratch((blocks + 1) * half, 2 * rows), split(4 * half), scratch((blocks + 1) * 4 * half, 2 * rows)],
    )
    arrived = exchange(leaving, order)
    wide = jax.ShapeDtypeStruct((rows, channels), jnp.bfloat16)
    return call(
        functools.partial(unpack_kernel, order, half),
        "unpack",
        [*arrived, gate, upstream],
        [wide, wide, wide, f32(rows, channels // 2)],
        [held],
    )


def pack_plain(signal, gate, taps, upstream, seqs, half):
    own = lax.axis_index("dp")
    by_owner = lambda value, parts: value.T.reshape(parts, -1, half, value.shape[0]).transpose(1, 0, 2, 3).reshape(-1, parts * half, value.shape[0])
    taps = lax.dynamic_slice_in_dim(taps, own * (taps.shape[1] // seqs), taps.shape[1] // seqs, 1)
    carried = upstream.astype(jnp.float32) * gate.astype(jnp.float32)
    return jnp.concatenate([by_owner(signal.astype(jnp.float32), seqs), by_owner(carried, seqs), by_owner(taps, 1)], axis=1)


def core_plain(arrived, blocks, seqs, half, scale):
    width = seqs * half
    rows = arrived.shape[-1]
    mine = arrived.reshape(blocks, seqs, (2 * seqs + 1) * half, rows)
    taps = mine[:, :, 2 * width :].reshape(blocks, 1, width, rows)
    columns = jnp.concatenate([mine[:, :, :width], mine[:, :, width : 2 * width], taps], axis=1)
    angle = 2.0 * np.pi * (np.outer(np.arange(blocks + 1), np.arange(blocks)) % (2 * blocks)) / (2 * blocks)
    cos_block, sin_block = jnp.asarray(np.cos(angle), jnp.float32), jnp.asarray(np.sin(angle), jnp.float32)
    cosine, sine = (jnp.asarray(table, jnp.float32)[:, None, None] for table in residue_table(blocks + 1, rows))
    table = jnp.asarray(block_table(rows), jnp.float32)
    einsum = functools.partial(jnp.einsum, precision=HIGHEST)
    real, imag = einsum("kp,pgct->kgct", cos_block, columns), -einsum("kp,pgct->kgct", sin_block, columns)
    real, imag = real * cosine + imag * sine, imag * cosine - real * sine
    spec = einsum("kgct,tf->kgcf", jnp.concatenate([real, imag], axis=-1), table)
    spec = lax.complex(spec[..., :rows], spec[..., rows:])
    x, carried, taps = spec[:, :seqs], spec[:, seqs : 2 * seqs], spec[:, 2 * seqs :]
    filt = jnp.sum(carried * jnp.conj(x), axis=1, keepdims=True) * scale
    spec = jnp.concatenate([x * taps, carried * jnp.conj(taps), filt], axis=1)
    back = einsum("kgct,tf->kgcf", jnp.concatenate([spec.real, -spec.imag], axis=-1), table)
    real, imag = back[..., :rows], -back[..., rows:]
    real, imag = real * cosine - imag * sine, imag * cosine + real * sine
    weight = np.full((blocks + 1, 1), 2.0)
    weight[0] = weight[-1] = 1.0
    weight = jnp.asarray(weight / (2 * blocks * rows), jnp.float32)
    out = einsum("kp,kgct->pgct", cos_block * weight, real) - einsum("kp,kgct->pgct", sin_block * weight, imag)
    filt = out[:, 2 * seqs :].reshape(blocks, seqs, half, rows)
    return jnp.concatenate([out[:, :seqs], out[:, seqs : 2 * seqs], filt], axis=2).reshape(arrived.shape)


def unpack_plain(arrived, gate, upstream, seqs, half):
    width = seqs * half
    whole = lambda value, parts: value.reshape(-1, parts, half, value.shape[-1]).transpose(1, 0, 2, 3).reshape(-1, value.shape[-1]).T
    convolved = whole(arrived[:, :width], seqs)
    return (
        (gate.astype(jnp.float32) * convolved).astype(jnp.bfloat16),
        (upstream.astype(jnp.float32) * convolved).astype(jnp.bfloat16),
        whole(arrived[:, width : 2 * width], seqs).astype(jnp.bfloat16),
        whole(arrived[:, 2 * width :], 1),
    )


def shards(hyena_input, gate_input, filter_taps, cotangent):
    signal, gate, upstream = hyena_input[0], gate_input[0], cotangent[0]
    rows, channels = signal.shape
    blocks, seqs = lax.axis_size("context"), lax.axis_size("dp")
    owners = blocks * seqs
    half = channels // owners // seqs
    scale = 1.0 / math.sqrt(seqs * blocks * rows)
    if seqs == 2 and blocks in (2, 4, 8) and rows == LANES and channels % (2 * LANES) == 0 and channels // blocks in (16, 32, 64, 128, 256):
        outputs = tiled_shards(signal, gate, filter_taps, upstream, blocks, channels // blocks // 2, scale)
    else:
        leaving = pack_plain(signal, gate, filter_taps, upstream, seqs, half)
        arrived = lax.all_to_all(leaving, ("context", "dp"), 0, 0, tiled=True)
        leaving = core_plain(arrived, blocks, seqs, half, scale)
        arrived = lax.all_to_all(leaving, ("context", "dp"), 0, 0, tiled=True)
        outputs = unpack_plain(arrived, gate, upstream, seqs, half)
    gated, gate_grad, input_grad, filter_grad = outputs
    return gated[None], gate_grad[None], input_grad[None], filter_grad


def solution(mesh):
    placed = P(("groups", "dp"), "context", None)
    return jax.shard_map(
        shards,
        mesh=mesh,
        in_specs=(placed, placed, P("context", "groups"), placed),
        out_specs=(placed, placed, placed, P("context", ("groups", "dp"))),
        check_vma=False,
    )
```

```python
import functools
import math

import jax
import jax.numpy as jnp
import numpy as np
from jax import lax
from jax.experimental import pallas as pl
from jax.experimental.pallas import tpu as pltpu
from jax.sharding import PartitionSpec as P

LANES = 128
LIMIT = 16 * 2**20
PARTS = 1
PACK_LIMIT = 53 * 2**20 + 2**18
ORDER = (4, 3, 5, 7, 2, 6, 1, 0)
ORDER_BACK = (4, 3, 5, 7, 2, 6, 1, 0)
HIGHEST = lax.Precision.HIGHEST


def block_table(rows):
    index = np.arange(rows)
    angle = 2.0 * np.pi * (np.outer(index, index) % rows) / rows
    cosine, sine = np.cos(angle), np.sin(angle)
    return np.block([[cosine, -sine], [sine, cosine]])


def residue_table(count, rows):
    angle = 2.0 * np.pi * np.outer(np.arange(count), np.arange(rows)) / (2 * (count - 1) * rows)
    return np.cos(angle), np.sin(angle)


def table_kernel(_, own_ref, table_ref, cos_ref, sin_ref, kept_ref):
    kept_ref[...] = own_ref[...]
    rows, count = cos_ref.shape[1], cos_ref.shape[0]
    grid = lambda height, axis: lax.broadcasted_iota(jnp.int32, (height, rows), axis)
    angle = (grid(rows, 0) * grid(rows, 1) % rows).astype(jnp.float32) * np.float32(2.0 * math.pi / rows)
    cosine, sine = jnp.cos(angle), jnp.sin(angle)
    for row, col, value in ((0, 0, cosine), (0, 1, -sine), (1, 0, sine), (1, 1, cosine)):
        high = value.astype(jnp.bfloat16)
        put = lambda part, piece: table_ref.__setitem__((pl.ds((2 * part + row) * rows, rows), pl.ds(col * rows, rows)), piece)
        put(0, high)
        put(1, high)
        put(2, (value - high.astype(jnp.float32)).astype(jnp.bfloat16))
    angle = (grid(count, 0) * grid(count, 1)).astype(jnp.float32) * np.float32(math.pi / ((count - 1) * rows))
    cos_ref[...] = jnp.cos(angle)
    sin_ref[...] = jnp.sin(angle)


def store_split(rows_ref, at, value):
    width = value.shape[1]
    high = value.astype(jnp.bfloat16)
    rows_ref[at, pl.ds(0, width)] = high
    rows_ref[at, pl.ds(width, width)] = (value - high.astype(jnp.float32)).astype(jnp.bfloat16)
    rows_ref[at, pl.ds(2 * width, width)] = high


def multiply(rows_ref, table_ref, out_ref, parts):
    size = rows_ref.shape[0] // parts
    for part in range(parts):
        at = pl.ds(part * size, size)
        out_ref[at, :] = jnp.dot(rows_ref[at, :], table_ref[...], preferred_element_type=jnp.float32)


def weighted(terms):
    total = None
    for weight, value in terms:
        if abs(weight) < 1e-12:
            continue
        if abs(weight - 1.0) < 1e-12:
            part = value
        elif abs(weight + 1.0) < 1e-12:
            total = -value if total is None else total - value
            continue
        else:
            part = value * np.float32(weight)
        total = part if total is None else total + part
    return total


def add(first, second):
    if first is None or second is None:
        return second if first is None else first
    return first + second


def sub(first, second):
    if second is None:
        return first
    return -second if first is None else first - second


def forward_sums(blocks, columns):
    turn = math.pi / blocks
    even, odd = range(0, blocks, 2), range(1, blocks, 2)
    sums = {}
    for k in range(blocks // 2 + 1):
        cos_even = weighted([(math.cos(turn * k * p), columns[p]) for p in even])
        cos_odd = weighted([(math.cos(turn * k * p), columns[p]) for p in odd])
        sin_even = weighted([(math.sin(turn * k * p), columns[p]) for p in even])
        sin_odd = weighted([(math.sin(turn * k * p), columns[p]) for p in odd])
        sums[k] = (add(cos_even, cos_odd), sub(sub(None, sin_even), sin_odd))
        if k != blocks - k:
            sums[blocks - k] = (sub(cos_even, cos_odd), sub(sin_even, sin_odd))
    return sums


def forward_rows(blocks, rows, load, cos_ref, sin_ref, rows_ref):
    for first in range(0, rows, 16):
        sums = forward_sums(blocks, [load(block, pl.ds(first, 16)) for block in range(blocks)])
        for k in range(blocks + 1):
            real, imag = sums[k]
            if k > 0:
                cosine, sine = cos_ref[pl.ds(k, 1), :], sin_ref[pl.ds(k, 1), :]
                if imag is None:
                    real, imag = real * cosine, -real * sine
                else:
                    real, imag = real * cosine + imag * sine, imag * cosine - real * sine
            imag = jnp.zeros_like(real) if imag is None else imag
            store_split(rows_ref, pl.ds(k * rows + first, 16), jnp.concatenate([real, imag], axis=1))


def times(first, second, conjugate):
    a, b, c, d = first[:, :LANES], first[:, LANES:], second[:, :LANES], second[:, LANES:]
    real, imag = (a * c + b * d, a * d - b * c) if conjugate else (a * c - b * d, -(a * d) - b * c)
    return jnp.concatenate([real, imag], axis=1)


def inverse_sums(blocks, rows, back_ref, cos_ref, sin_ref, put):
    turn = math.pi / blocks
    scale = 1.0 / (2 * blocks * LANES)
    for first in range(0, rows, 8):
        real, imag = [], [None] * (blocks + 1)
        for k in range(blocks + 1):
            at = pl.ds(k * rows + first, 8)
            weight = np.float32(scale if k in (0, blocks) else 2.0 * scale)
            one = back_ref[at, pl.ds(0, LANES)] * weight
            if k > 0:
                other = back_ref[at, pl.ds(LANES, LANES)] * weight
                cosine, sine = cos_ref[pl.ds(k, 1), :], sin_ref[pl.ds(k, 1), :]
                if k < blocks:
                    imag[k] = one * sine - other * cosine
                one = one * cosine + other * sine
            real.append(one)
        for block in range(blocks // 2 + 1):
            cos_even = weighted([(math.cos(turn * k * block), real[k]) for k in range(0, blocks + 1, 2)])
            cos_odd = weighted([(math.cos(turn * k * block), real[k]) for k in range(1, blocks, 2)])
            sin_even = weighted([(math.sin(turn * k * block), imag[k]) for k in range(2, blocks, 2)])
            sin_odd = weighted([(math.sin(turn * k * block), imag[k]) for k in range(1, blocks, 2)])
            put(block, first, sub(sub(add(cos_even, cos_odd), sin_even), sin_odd))
            if block not in (0, blocks - block):
                put(blocks - block, first, sub(add(sub(cos_even, cos_odd), sin_even), sin_odd))


def gather_kernel(order, half, *refs):
    me = lax.axis_index("context")
    for step, block_ref in zip(order, refs[:-1]):
        refs[-1][me ^ step] = block_ref[pl.ds(4 * half, half), :]


def analyse_kernel(order, half, scale, *refs):
    blocks, size = len(order), 5 * half
    block_refs, (table_ref, cos_ref, sin_ref, spec_ref, keep_ref, swap_ref, held_ref, in_ref, out_ref, back_ref) = refs[:blocks], refs[blocks:]
    me = lax.axis_index("context")
    for step, block_ref in zip(order, block_refs):
        held_ref[me ^ step] = block_ref[...]
    forward_rows(blocks, size, lambda block, at: held_ref[block, at, :], cos_ref, sin_ref, in_ref)
    multiply(in_ref, table_ref, spec_ref, PARTS)
    for k in range(blocks + 1):
        for first in range(0, 2 * half, 16):
            at = lambda part: pl.ds(k * size + 2 * half * part + first, 16)
            store_split(out_ref, pl.ds(k * 2 * half + first, 16), times(spec_ref[at(1), :], spec_ref[at(0), :], True) * scale)
    multiply(out_ref, table_ref, back_ref, PARTS)

    def put(block, first, value):
        if first < half:
            keep_ref[block, pl.ds(first, 8), :] = value
        else:
            swap_ref[block, pl.ds(first - half, 8), :] = value

    inverse_sums(blocks, 2 * half, back_ref, cos_ref, sin_ref, put)


def combine_kernel(blocks, half, spec_ref, swapped_ref, table_ref, cos_ref, sin_ref, held_ref, in_ref, taps_ref, out_ref, back_ref):
    size = 5 * half
    forward_rows(blocks, half, lambda block, at: swapped_ref[block, at, :], cos_ref, sin_ref, in_ref)
    multiply(in_ref, table_ref, taps_ref, 1)
    for k in range(blocks + 1):
        for first in range(0, 2 * half, 16):
            taps = spec_ref[pl.ds(k * size + 4 * half + first, 16), :] if first < half else taps_ref[pl.ds(k * half + first - half, 16), :]
            for part in range(2):
                spec = spec_ref[pl.ds(k * size + 2 * half * part + first, 16), :]
                store_split(out_ref, pl.ds(k * 4 * half + 2 * half * part + first, 16), times(spec, taps, part == 1))
    multiply(out_ref, table_ref, back_ref, PARTS)

    def put(block, first, value):
        held_ref[block, pl.ds(first, 8), :] = value

    inverse_sums(blocks, 4 * half, back_ref, cos_ref, sin_ref, put)


def finish_kernel(order, half, held_ref, keep_ref, swapped_ref, *block_refs):
    me = lax.axis_index("context")
    for step, block_ref in zip(order, block_refs):
        block_ref[pl.ds(0, 4 * half), :] = held_ref[me ^ step]
        block_ref[pl.ds(4 * half, half), :] = keep_ref[me ^ step] + swapped_ref[me ^ step]


def lanes_of(tile, per_half):
    start = (lax.axis_index("dp") ^ (tile // per_half)) * (per_half * LANES) + tile % per_half * LANES
    return pl.ds(pl.multiple_of(start, LANES), LANES)


def pack_kernel(order, half, *refs):
    blocks = len(order)
    signal_hbm, gate_hbm, taps_hbm, upstream_hbm = refs[:4]
    block_refs, (held_ref, signal_ref, gate_ref, taps_ref, upstream_ref, arrived) = refs[4 : 4 + blocks], refs[4 + blocks :]
    group = LANES // half
    per_half = signal_ref.shape[1] // 2 // LANES
    own = pl.ds(pl.multiple_of(lax.axis_index("dp") * (per_half * LANES), LANES), per_half * LANES)
    pairs = [(upstream_hbm, upstream_ref), (gate_hbm, gate_ref), (signal_hbm, signal_ref), (taps_hbm.at[:, own], taps_ref)]
    copies = [pltpu.make_async_copy(*pair, arrived.at[i]) for i, pair in enumerate(pairs)]
    for copy in copies:
        copy.start()

    def store(tile, row, value):
        held_ref[pl.ds(tile % per_half * group, group), pl.ds(row, half), :] = value.T.reshape(group, half, LANES)

    for copy in copies[:2]:
        copy.wait()
    for tile in range(2 * per_half):
        lanes = lanes_of(tile, per_half)
        carried = upstream_ref[:, lanes].astype(jnp.float32) * gate_ref[:, lanes].astype(jnp.float32)
        store(tile, (2 + tile // per_half) * half, carried)
    copies[2].wait()
    for tile in range(2 * per_half):
        store(tile, tile // per_half * half, signal_ref[:, lanes_of(tile, per_half)].astype(jnp.float32))
    copies[3].wait()
    for tile in range(per_half):
        store(tile, 4 * half, taps_ref[:, pl.ds(tile * LANES, LANES)])
    me = lax.axis_index("context")
    for step, block_ref in zip(order, block_refs):
        block_ref[...] = held_ref[me ^ step]


def unpack_kernel(order, half, *refs):
    blocks = len(order)
    block_refs, (gate_ref, upstream_ref, gated_ref, gate_grad_ref, input_grad_ref, filter_grad_ref, held_ref) = refs[:blocks], refs[blocks:]
    me = lax.axis_index("context")
    for step, block_ref in zip(order, block_refs):
        held_ref[me ^ step] = block_ref[...]
    group = LANES // half
    per_half = gate_ref.shape[1] // 2 // LANES
    for tile in range(2 * per_half):
        lanes = lanes_of(tile, per_half)
        of, row = pl.ds(tile % per_half * group, group), tile // per_half * half
        convolved = held_ref[of, pl.ds(row, half), :].reshape(LANES, LANES).T
        gated_ref[:, lanes] = (gate_ref[:, lanes].astype(jnp.float32) * convolved).astype(jnp.bfloat16)
        gate_grad_ref[:, lanes] = (upstream_ref[:, lanes].astype(jnp.float32) * convolved).astype(jnp.bfloat16)
        input_grad_ref[:, lanes] = held_ref[of, pl.ds(2 * half + row, half), :].reshape(LANES, LANES).T.astype(jnp.bfloat16)
        if tile < per_half:
            filter_grad_ref[:, pl.ds(tile * LANES, LANES)] = held_ref[of, pl.ds(4 * half, half), :].reshape(LANES, LANES).T


def exchange(parts, order):
    devices = lax.axis_size("context")
    send = lambda part, step: lax.ppermute(part, "context", [(place, place ^ step) for place in range(devices)])
    return [part if step == 0 else send(part, step) for part, step in zip(parts, order)]


def tiled_shards(signal, gate, taps, upstream, blocks, half, scale):
    rows, channels = signal.shape
    order, order_back = ([step for step in steps if step < blocks] for steps in (ORDER, ORDER_BACK))
    f32 = lambda *shape: jax.ShapeDtypeStruct(shape, jnp.float32)
    scratch = lambda *shape: pltpu.VMEM(shape, jnp.float32)
    split = lambda count: pltpu.VMEM(((blocks + 1) * count, 6 * rows), jnp.bfloat16)

    def call(kernel, name, inputs, outputs, scratches, space=pltpu.VMEM, limit=LIMIT):
        return pl.pallas_call(
            kernel,
            out_shape=outputs,
            in_specs=[pl.BlockSpec(memory_space=space)] * len(inputs),
            out_specs=[pl.BlockSpec(memory_space=pltpu.VMEM)] * len(outputs),
            scratch_shapes=scratches,
            compiler_params=pltpu.CompilerParams(vmem_limit_bytes=limit),
            name=name,
        )(*inputs)

    size = 5 * half
    held = scratch(blocks, size, rows)
    narrow = lambda *shape: pltpu.VMEM(shape, jnp.bfloat16)
    leaving = call(
        functools.partial(pack_kernel, order, half),
        "pack",
        [signal, gate, taps, upstream],
        [f32(size, rows)] * blocks,
        [held, narrow(rows, channels), narrow(rows, channels), scratch(rows, channels // 2), narrow(rows, channels), pltpu.SemaphoreType.DMA((4,))],
        pltpu.HBM,
        PACK_LIMIT,
    )
    arrived = exchange(leaving, order)
    *tables, arrived[-1] = call(
        table_kernel,
        "tables",
        [arrived[0], arrived[-1]],
        [jax.ShapeDtypeStruct((6 * rows, 2 * rows), jnp.bfloat16), f32(blocks + 1, rows), f32(blocks + 1, rows), f32(size, rows)],
        [],
    )
    swap = lambda part: lax.ppermute(part, "dp", [(0, 1), (1, 0)])
    other_taps = swap(call(functools.partial(gather_kernel, order, half), "gather", arrived, [f32(blocks, half, rows)], [])[0])
    spec, keep, partial_sum = call(
        functools.partial(analyse_kernel, order, half, np.float32(scale)),
        "analyse",
        [*arrived, *tables],
        [f32((blocks + 1) * size, 2 * rows), f32(blocks, half, rows), f32(blocks, half, rows)],
        [held, split(size), split(2 * half), scratch((blocks + 1) * 2 * half, 2 * rows)],
    )
    partial_sum = swap(partial_sum)
    [both] = call(
        functools.partial(combine_kernel, blocks, half),
        "combine",
        [spec, other_taps, *tables],
        [f32(blocks, 4 * half, rows)],
        [split(half), scratch((blocks + 1) * half, 2 * rows), split(4 * half), scratch((blocks + 1) * 4 * half, 2 * rows)],
    )
    leaving = call(functools.partial(finish_kernel, order_back, half), "finish", [both, keep, partial_sum], [f32(size, rows)] * blocks, [])
    arrived = exchange(leaving, order_back)
    wide = jax.ShapeDtypeStruct((rows, channels), jnp.bfloat16)
    return call(
        functools.partial(unpack_kernel, order_back, half),
        "unpack",
        [*arrived, gate, upstream],
        [wide, wide, wide, f32(rows, channels // 2)],
        [held],
    )


def pack_plain(signal, gate, taps, upstream, seqs, half):
    own = lax.axis_index("dp")
    by_owner = lambda value, parts: value.T.reshape(parts, -1, half, value.shape[0]).transpose(1, 0, 2, 3).reshape(-1, parts * half, value.shape[0])
    taps = lax.dynamic_slice_in_dim(taps, own * (taps.shape[1] // seqs), taps.shape[1] // seqs, 1)
    carried = upstream.astype(jnp.float32) * gate.astype(jnp.float32)
    return jnp.concatenate([by_owner(signal.astype(jnp.float32), seqs), by_owner(carried, seqs), by_owner(taps, 1)], axis=1)


def core_plain(arrived, blocks, seqs, half, scale):
    width = seqs * half
    rows = arrived.shape[-1]
    mine = arrived.reshape(blocks, seqs, (2 * seqs + 1) * half, rows)
    taps = mine[:, :, 2 * width :].reshape(blocks, 1, width, rows)
    columns = jnp.concatenate([mine[:, :, :width], mine[:, :, width : 2 * width], taps], axis=1)
    angle = 2.0 * np.pi * (np.outer(np.arange(blocks + 1), np.arange(blocks)) % (2 * blocks)) / (2 * blocks)
    cos_block, sin_block = jnp.asarray(np.cos(angle), jnp.float32), jnp.asarray(np.sin(angle), jnp.float32)
    cosine, sine = (jnp.asarray(table, jnp.float32)[:, None, None] for table in residue_table(blocks + 1, rows))
    table = jnp.asarray(block_table(rows), jnp.float32)
    einsum = functools.partial(jnp.einsum, precision=HIGHEST)
    real, imag = einsum("kp,pgct->kgct", cos_block, columns), -einsum("kp,pgct->kgct", sin_block, columns)
    real, imag = real * cosine + imag * sine, imag * cosine - real * sine
    spec = einsum("kgct,tf->kgcf", jnp.concatenate([real, imag], axis=-1), table)
    spec = lax.complex(spec[..., :rows], spec[..., rows:])
    x, carried, taps = spec[:, :seqs], spec[:, seqs : 2 * seqs], spec[:, 2 * seqs :]
    filt = jnp.sum(carried * jnp.conj(x), axis=1, keepdims=True) * scale
    spec = jnp.concatenate([x * taps, carried * jnp.conj(taps), filt], axis=1)
    back = einsum("kgct,tf->kgcf", jnp.concatenate([spec.real, -spec.imag], axis=-1), table)
    real, imag = back[..., :rows], -back[..., rows:]
    real, imag = real * cosine - imag * sine, imag * cosine + real * sine
    weight = np.full((blocks + 1, 1), 2.0)
    weight[0] = weight[-1] = 1.0
    weight = jnp.asarray(weight / (2 * blocks * rows), jnp.float32)
    out = einsum("kp,kgct->pgct", cos_block * weight, real) - einsum("kp,kgct->pgct", sin_block * weight, imag)
    filt = out[:, 2 * seqs :].reshape(blocks, seqs, half, rows)
    return jnp.concatenate([out[:, :seqs], out[:, seqs : 2 * seqs], filt], axis=2).reshape(arrived.shape)


def unpack_plain(arrived, gate, upstream, seqs, half):
    width = seqs * half
    whole = lambda value, parts: value.reshape(-1, parts, half, value.shape[-1]).transpose(1, 0, 2, 3).reshape(-1, value.shape[-1]).T
    convolved = whole(arrived[:, :width], seqs)
    return (
        (gate.astype(jnp.float32) * convolved).astype(jnp.bfloat16),
        (upstream.astype(jnp.float32) * convolved).astype(jnp.bfloat16),
        whole(arrived[:, width : 2 * width], seqs).astype(jnp.bfloat16),
        whole(arrived[:, 2 * width :], 1),
    )


def shards(hyena_input, gate_input, filter_taps, cotangent):
    signal, gate, upstream = hyena_input[0], gate_input[0], cotangent[0]
    rows, channels = signal.shape
    blocks, seqs = lax.axis_size("context"), lax.axis_size("dp")
    owners = blocks * seqs
    half = channels // owners // seqs
    scale = 1.0 / math.sqrt(seqs * blocks * rows)
    if seqs == 2 and blocks in (2, 4, 8) and rows == LANES and channels % (2 * LANES) == 0 and channels // blocks in (16, 32, 64, 128, 256):
        outputs = tiled_shards(signal, gate, filter_taps, upstream, blocks, channels // blocks // 2, scale)
    else:
        leaving = pack_plain(signal, gate, filter_taps, upstream, seqs, half)
        arrived = lax.all_to_all(leaving, ("context", "dp"), 0, 0, tiled=True)
        leaving = core_plain(arrived, blocks, seqs, half, scale)
        arrived = lax.all_to_all(leaving, ("context", "dp"), 0, 0, tiled=True)
        outputs = unpack_plain(arrived, gate, upstream, seqs, half)
    gated, gate_grad, input_grad, filter_grad = outputs
    return gated[None], gate_grad[None], input_grad[None], filter_grad


def solution(mesh):
    placed = P(("groups", "dp"), "context", None)
    return jax.shard_map(
        shards,
        mesh=mesh,
        in_specs=(placed, placed, P("context", "groups"), placed),
        out_specs=(placed, placed, placed, P("context", ("groups", "dp"))),
        check_vma=False,
    )
```

```python
import functools
import math

import jax
import jax.numpy as jnp
import numpy as np
from jax import lax
from jax.experimental import pallas as pl
from jax.experimental.pallas import tpu as pltpu
from jax.sharding import PartitionSpec as P

LANES = 128
LIMIT = 16 * 2**20
PACK_LIMIT = 53 * 2**20 + 2**18
ORDER = (4, 2, 5, 7, 3, 6, 1, 0)
ORDER_BACK = (4, 3, 5, 7, 2, 6, 1, 0)
HIGHEST = lax.Precision.HIGHEST


def block_table(rows):
    index = np.arange(rows)
    angle = 2.0 * np.pi * (np.outer(index, index) % rows) / rows
    cosine, sine = np.cos(angle), np.sin(angle)
    return np.block([[cosine, -sine], [sine, cosine]])


def residue_table(count, rows):
    angle = 2.0 * np.pi * np.outer(np.arange(count), np.arange(rows)) / (2 * (count - 1) * rows)
    return np.cos(angle), np.sin(angle)


def table_kernel(_, own_ref, table_ref, cos_ref, sin_ref, kept_ref):
    kept_ref[...] = own_ref[...]
    rows, count = cos_ref.shape[1], cos_ref.shape[0]
    grid = lambda height, axis: lax.broadcasted_iota(jnp.int32, (height, rows), axis)
    angle = (grid(rows, 0) * grid(rows, 1) % rows).astype(jnp.float32) * np.float32(2.0 * math.pi / rows)
    cosine, sine = jnp.cos(angle), jnp.sin(angle)
    for row, col, value in ((0, 0, cosine), (0, 1, -sine), (1, 0, sine), (1, 1, cosine)):
        high = value.astype(jnp.bfloat16)
        put = lambda part, piece: table_ref.__setitem__((pl.ds((2 * part + row) * rows, rows), pl.ds(col * rows, rows)), piece)
        put(0, high)
        put(1, high)
        put(2, (value - high.astype(jnp.float32)).astype(jnp.bfloat16))
    angle = (grid(count, 0) * grid(count, 1)).astype(jnp.float32) * np.float32(math.pi / ((count - 1) * rows))
    cos_ref[...] = jnp.cos(angle)
    sin_ref[...] = jnp.sin(angle)


def store_split(rows_ref, at, value):
    width = value.shape[1]
    high = value.astype(jnp.bfloat16)
    rows_ref[at, pl.ds(0, width)] = high
    rows_ref[at, pl.ds(width, width)] = (value - high.astype(jnp.float32)).astype(jnp.bfloat16)
    rows_ref[at, pl.ds(2 * width, width)] = high


def multiply(rows_ref, table_ref, out_ref, base, size):
    at = pl.ds(base, size)
    out_ref[at, :] = jnp.dot(rows_ref[at, :], table_ref[...], preferred_element_type=jnp.float32)


def weighted(terms):
    total = None
    for weight, value in terms:
        if abs(weight) < 1e-12:
            continue
        if abs(weight - 1.0) < 1e-12:
            part = value
        elif abs(weight + 1.0) < 1e-12:
            total = -value if total is None else total - value
            continue
        else:
            part = value * np.float32(weight)
        total = part if total is None else total + part
    return total


def add(first, second):
    if first is None or second is None:
        return second if first is None else first
    return first + second


def sub(first, second):
    if second is None:
        return first
    return -second if first is None else first - second


def forward_sums(blocks, columns):
    turn = math.pi / blocks
    even, odd = range(0, blocks, 2), range(1, blocks, 2)
    sums = {}
    for k in range(blocks // 2 + 1):
        cos_even = weighted([(math.cos(turn * k * p), columns[p]) for p in even])
        cos_odd = weighted([(math.cos(turn * k * p), columns[p]) for p in odd])
        sin_even = weighted([(math.sin(turn * k * p), columns[p]) for p in even])
        sin_odd = weighted([(math.sin(turn * k * p), columns[p]) for p in odd])
        sums[k] = (add(cos_even, cos_odd), sub(sub(None, sin_even), sin_odd))
        if k != blocks - k:
            sums[blocks - k] = (sub(cos_even, cos_odd), sub(sin_even, sin_odd))
    return sums


def forward_rows(blocks, sources, load, cos_ref, sin_ref, rows_ref, base):
    rows = 16 * len(sources)
    for first, source in zip(range(0, rows, 16), sources):
        sums = forward_sums(blocks, [load(block, pl.ds(source, 16)) for block in range(blocks)])
        for k in range(blocks + 1):
            real, imag = sums[k]
            if k > 0:
                cosine, sine = cos_ref[pl.ds(k, 1), :], sin_ref[pl.ds(k, 1), :]
                if imag is None:
                    real, imag = real * cosine, -real * sine
                else:
                    real, imag = real * cosine + imag * sine, imag * cosine - real * sine
            imag = jnp.zeros_like(real) if imag is None else imag
            store_split(rows_ref, pl.ds(base + k * rows + first, 16), jnp.concatenate([real, imag], axis=1))


def times(first, second, conjugate):
    a, b, c, d = first[:, :LANES], first[:, LANES:], second[:, :LANES], second[:, LANES:]
    real, imag = (a * c + b * d, a * d - b * c) if conjugate else (a * c - b * d, -(a * d) - b * c)
    return jnp.concatenate([real, imag], axis=1)


def inverse_sums(blocks, rows, back_ref, base, cos_ref, sin_ref, put):
    turn = math.pi / blocks
    scale = 1.0 / (2 * blocks * LANES)
    for first in range(0, rows, 8):
        real, imag = [], [None] * (blocks + 1)
        for k in range(blocks + 1):
            at = pl.ds(base + k * rows + first, 8)
            weight = np.float32(scale if k in (0, blocks) else 2.0 * scale)
            one = back_ref[at, pl.ds(0, LANES)] * weight
            if k > 0:
                other = back_ref[at, pl.ds(LANES, LANES)] * weight
                cosine, sine = cos_ref[pl.ds(k, 1), :], sin_ref[pl.ds(k, 1), :]
                if k < blocks:
                    imag[k] = one * sine - other * cosine
                one = one * cosine + other * sine
            real.append(one)
        for block in range(blocks // 2 + 1):
            cos_even = weighted([(math.cos(turn * k * block), real[k]) for k in range(0, blocks + 1, 2)])
            cos_odd = weighted([(math.cos(turn * k * block), real[k]) for k in range(1, blocks, 2)])
            sin_even = weighted([(math.sin(turn * k * block), imag[k]) for k in range(2, blocks, 2)])
            sin_odd = weighted([(math.sin(turn * k * block), imag[k]) for k in range(1, blocks, 2)])
            put(block, first, sub(sub(add(cos_even, cos_odd), sin_even), sin_odd))
            if block not in (0, blocks - block):
                put(blocks - block, first, sub(add(sub(cos_even, cos_odd), sin_even), sin_odd))


def gather_kernel(order, half, *refs):
    me = lax.axis_index("context")
    for step, block_ref in zip(order, refs[:-1]):
        refs[-1][me ^ step] = block_ref[pl.ds(4 * half, half), :]


def analyse_kernel(order, half, scale, *refs):
    blocks = len(order)
    block_refs, (table_ref, cos_ref, sin_ref, spec_ref, keep_ref, swap_ref, held_ref, in_ref, out_ref, back_ref) = refs[:blocks], refs[blocks:]
    me = lax.axis_index("context")
    for step, block_ref in zip(order, block_refs):
        held_ref[me ^ step] = block_ref[...]
    load = lambda block, at: held_ref[block, at, :]
    cells = (blocks + 1) * half

    def forward(group):
        starts = [4 * half] if group == 2 else [group * half, (2 + group) * half]
        sources = [start + row for start in starts for row in range(0, half, 16)]
        forward_rows(blocks, sources, load, cos_ref, sin_ref, in_ref, 2 * group * cells)
        multiply(in_ref, table_ref, spec_ref, 2 * group * cells, len(starts) * cells)

    def back(group):
        for k in range(blocks + 1):
            for first in range(0, half, 16):
                at = lambda part: pl.ds(2 * group * cells + (2 * k + part) * half + first, 16)
                store_split(out_ref, pl.ds(group * cells + k * half + first, 16), times(spec_ref[at(1), :], spec_ref[at(0), :], True) * scale)
        multiply(out_ref, table_ref, back_ref, group * cells, cells)

    def finish(group, to_ref):
        def put(block, first, value):
            to_ref[block, pl.ds(first, 8), :] = value

        inverse_sums(blocks, half, back_ref, group * cells, cos_ref, sin_ref, put)

    forward(1)
    forward(0)
    back(1)
    forward(2)
    back(0)
    finish(1, swap_ref)
    finish(0, keep_ref)


def combine_kernel(blocks, half, spec_ref, swapped_ref, table_ref, cos_ref, sin_ref, held_ref, in_ref, taps_ref, out_ref, back_ref):
    cells = (blocks + 1) * half

    def back(group, taps_at):
        for k in range(blocks + 1):
            for first in range(0, half, 16):
                taps = taps_at(k * half + first)
                for part in range(2):
                    at = pl.ds(2 * group * cells + (2 * k + part) * half + first, 16)
                    store_split(out_ref, at, times(spec_ref[at, :], taps, part == 1))
        multiply(out_ref, table_ref, back_ref, 2 * group * cells, 2 * cells)

    def finish(group):
        def put(block, first, value):
            held_ref[block, pl.ds((2 * (first // half) + group) * half + first % half, 8), :] = value

        inverse_sums(blocks, 2 * half, back_ref, 2 * group * cells, cos_ref, sin_ref, put)

    forward_rows(blocks, range(0, half, 16), lambda block, at: swapped_ref[block, at, :], cos_ref, sin_ref, in_ref, 0)
    multiply(in_ref, table_ref, taps_ref, 0, cells)
    back(0, lambda row: spec_ref[pl.ds(4 * cells + row, 16), :])
    back(1, lambda row: taps_ref[pl.ds(row, 16), :])
    finish(0)
    finish(1)


def finish_kernel(order, half, held_ref, keep_ref, swapped_ref, *block_refs):
    me = lax.axis_index("context")
    for step, block_ref in zip(order, block_refs):
        block_ref[pl.ds(0, 4 * half), :] = held_ref[me ^ step]
        block_ref[pl.ds(4 * half, half), :] = keep_ref[me ^ step] + swapped_ref[me ^ step]


def lanes_of(tile, per_half):
    start = (lax.axis_index("dp") ^ (tile // per_half)) * (per_half * LANES) + tile % per_half * LANES
    return pl.ds(pl.multiple_of(start, LANES), LANES)


def pack_kernel(order, half, *refs):
    blocks = len(order)
    signal_hbm, gate_hbm, taps_hbm, upstream_hbm = refs[:4]
    block_refs, (held_ref, signal_ref, gate_ref, taps_ref, upstream_ref, arrived) = refs[4 : 4 + blocks], refs[4 + blocks :]
    group = LANES // half
    per_half = signal_ref.shape[1] // 2 // LANES
    own = pl.ds(pl.multiple_of(lax.axis_index("dp") * (per_half * LANES), LANES), per_half * LANES)
    pairs = [(upstream_hbm, upstream_ref), (gate_hbm, gate_ref), (signal_hbm, signal_ref), (taps_hbm.at[:, own], taps_ref)]
    copies = [pltpu.make_async_copy(*pair, arrived.at[i]) for i, pair in enumerate(pairs)]
    for copy in copies:
        copy.start()

    def store(tile, row, value):
        held_ref[pl.ds(tile % per_half * group, group), pl.ds(row, half), :] = value.T.reshape(group, half, LANES)

    for copy in copies[:2]:
        copy.wait()
    for tile in range(2 * per_half):
        lanes = lanes_of(tile, per_half)
        carried = upstream_ref[:, lanes].astype(jnp.float32) * gate_ref[:, lanes].astype(jnp.float32)
        store(tile, (2 + tile // per_half) * half, carried)
    copies[2].wait()
    for tile in range(2 * per_half):
        store(tile, tile // per_half * half, signal_ref[:, lanes_of(tile, per_half)].astype(jnp.float32))
    copies[3].wait()
    for tile in range(per_half):
        store(tile, 4 * half, taps_ref[:, pl.ds(tile * LANES, LANES)])
    me = lax.axis_index("context")
    for step, block_ref in zip(order, block_refs):
        block_ref[...] = held_ref[me ^ step]


def unpack_kernel(order, half, *refs):
    blocks = len(order)
    block_refs, (gate_ref, upstream_ref, gated_ref, gate_grad_ref, input_grad_ref, filter_grad_ref, held_ref) = refs[:blocks], refs[blocks:]
    me = lax.axis_index("context")
    for step, block_ref in zip(order, block_refs):
        held_ref[me ^ step] = block_ref[...]
    group = LANES // half
    per_half = gate_ref.shape[1] // 2 // LANES
    for tile in range(2 * per_half):
        lanes = lanes_of(tile, per_half)
        of, row = pl.ds(tile % per_half * group, group), tile // per_half * half
        convolved = held_ref[of, pl.ds(row, half), :].reshape(LANES, LANES).T
        gated_ref[:, lanes] = (gate_ref[:, lanes].astype(jnp.float32) * convolved).astype(jnp.bfloat16)
        gate_grad_ref[:, lanes] = (upstream_ref[:, lanes].astype(jnp.float32) * convolved).astype(jnp.bfloat16)
        input_grad_ref[:, lanes] = held_ref[of, pl.ds(2 * half + row, half), :].reshape(LANES, LANES).T.astype(jnp.bfloat16)
        if tile < per_half:
            filter_grad_ref[:, pl.ds(tile * LANES, LANES)] = held_ref[of, pl.ds(4 * half, half), :].reshape(LANES, LANES).T


def exchange(parts, order):
    devices = lax.axis_size("context")
    send = lambda part, step: lax.ppermute(part, "context", [(place, place ^ step) for place in range(devices)])
    return [part if step == 0 else send(part, step) for part, step in zip(parts, order)]


def tiled_shards(signal, gate, taps, upstream, blocks, half, scale):
    rows, channels = signal.shape
    order, order_back = ([step for step in steps if step < blocks] for steps in (ORDER, ORDER_BACK))
    f32 = lambda *shape: jax.ShapeDtypeStruct(shape, jnp.float32)
    scratch = lambda *shape: pltpu.VMEM(shape, jnp.float32)
    split = lambda count: pltpu.VMEM(((blocks + 1) * count, 6 * rows), jnp.bfloat16)

    def call(kernel, name, inputs, outputs, scratches, space=pltpu.VMEM, limit=LIMIT):
        return pl.pallas_call(
            kernel,
            out_shape=outputs,
            in_specs=[pl.BlockSpec(memory_space=space)] * len(inputs),
            out_specs=[pl.BlockSpec(memory_space=pltpu.VMEM)] * len(outputs),
            scratch_shapes=scratches,
            compiler_params=pltpu.CompilerParams(vmem_limit_bytes=limit),
            name=name,
        )(*inputs)

    size = 5 * half
    held = scratch(blocks, size, rows)
    narrow = lambda *shape: pltpu.VMEM(shape, jnp.bfloat16)
    leaving = call(
        functools.partial(pack_kernel, order, half),
        "pack",
        [signal, gate, taps, upstream],
        [f32(size, rows)] * blocks,
        [held, narrow(rows, channels), narrow(rows, channels), scratch(rows, channels // 2), narrow(rows, channels), pltpu.SemaphoreType.DMA((4,))],
        pltpu.HBM,
        PACK_LIMIT,
    )
    arrived = exchange(leaving, order)
    *tables, arrived[-1] = call(
        table_kernel,
        "tables",
        [arrived[0], arrived[-1]],
        [jax.ShapeDtypeStruct((6 * rows, 2 * rows), jnp.bfloat16), f32(blocks + 1, rows), f32(blocks + 1, rows), f32(size, rows)],
        [],
    )
    swap = lambda part: lax.ppermute(part, "dp", [(0, 1), (1, 0)])
    other_taps = swap(call(functools.partial(gather_kernel, order, half), "gather", arrived, [f32(blocks, half, rows)], [])[0])
    spec, keep, partial_sum = call(
        functools.partial(analyse_kernel, order, half, np.float32(scale)),
        "analyse",
        [*arrived, *tables],
        [f32((blocks + 1) * size, 2 * rows), f32(blocks, half, rows), f32(blocks, half, rows)],
        [held, split(size), split(2 * half), scratch((blocks + 1) * 2 * half, 2 * rows)],
    )
    partial_sum = swap(partial_sum)
    [both] = call(
        functools.partial(combine_kernel, blocks, half),
        "combine",
        [spec, other_taps, *tables],
        [f32(blocks, 4 * half, rows)],
        [split(half), scratch((blocks + 1) * half, 2 * rows), split(4 * half), scratch((blocks + 1) * 4 * half, 2 * rows)],
    )
    leaving = call(functools.partial(finish_kernel, order_back, half), "finish", [both, keep, partial_sum], [f32(size, rows)] * blocks, [])
    arrived = exchange(leaving, order_back)
    wide = jax.ShapeDtypeStruct((rows, channels), jnp.bfloat16)
    return call(
        functools.partial(unpack_kernel, order_back, half),
        "unpack",
        [*arrived, gate, upstream],
        [wide, wide, wide, f32(rows, channels // 2)],
        [held],
    )


def pack_plain(signal, gate, taps, upstream, seqs, half):
    own = lax.axis_index("dp")
    by_owner = lambda value, parts: value.T.reshape(parts, -1, half, value.shape[0]).transpose(1, 0, 2, 3).reshape(-1, parts * half, value.shape[0])
    taps = lax.dynamic_slice_in_dim(taps, own * (taps.shape[1] // seqs), taps.shape[1] // seqs, 1)
    carried = upstream.astype(jnp.float32) * gate.astype(jnp.float32)
    return jnp.concatenate([by_owner(signal.astype(jnp.float32), seqs), by_owner(carried, seqs), by_owner(taps, 1)], axis=1)


def core_plain(arrived, blocks, seqs, half, scale):
    width = seqs * half
    rows = arrived.shape[-1]
    mine = arrived.reshape(blocks, seqs, (2 * seqs + 1) * half, rows)
    taps = mine[:, :, 2 * width :].reshape(blocks, 1, width, rows)
    columns = jnp.concatenate([mine[:, :, :width], mine[:, :, width : 2 * width], taps], axis=1)
    angle = 2.0 * np.pi * (np.outer(np.arange(blocks + 1), np.arange(blocks)) % (2 * blocks)) / (2 * blocks)
    cos_block, sin_block = jnp.asarray(np.cos(angle), jnp.float32), jnp.asarray(np.sin(angle), jnp.float32)
    cosine, sine = (jnp.asarray(table, jnp.float32)[:, None, None] for table in residue_table(blocks + 1, rows))
    table = jnp.asarray(block_table(rows), jnp.float32)
    einsum = functools.partial(jnp.einsum, precision=HIGHEST)
    real, imag = einsum("kp,pgct->kgct", cos_block, columns), -einsum("kp,pgct->kgct", sin_block, columns)
    real, imag = real * cosine + imag * sine, imag * cosine - real * sine
    spec = einsum("kgct,tf->kgcf", jnp.concatenate([real, imag], axis=-1), table)
    spec = lax.complex(spec[..., :rows], spec[..., rows:])
    x, carried, taps = spec[:, :seqs], spec[:, seqs : 2 * seqs], spec[:, 2 * seqs :]
    filt = jnp.sum(carried * jnp.conj(x), axis=1, keepdims=True) * scale
    spec = jnp.concatenate([x * taps, carried * jnp.conj(taps), filt], axis=1)
    back = einsum("kgct,tf->kgcf", jnp.concatenate([spec.real, -spec.imag], axis=-1), table)
    real, imag = back[..., :rows], -back[..., rows:]
    real, imag = real * cosine - imag * sine, imag * cosine + real * sine
    weight = np.full((blocks + 1, 1), 2.0)
    weight[0] = weight[-1] = 1.0
    weight = jnp.asarray(weight / (2 * blocks * rows), jnp.float32)
    out = einsum("kp,kgct->pgct", cos_block * weight, real) - einsum("kp,kgct->pgct", sin_block * weight, imag)
    filt = out[:, 2 * seqs :].reshape(blocks, seqs, half, rows)
    return jnp.concatenate([out[:, :seqs], out[:, seqs : 2 * seqs], filt], axis=2).reshape(arrived.shape)


def unpack_plain(arrived, gate, upstream, seqs, half):
    width = seqs * half
    whole = lambda value, parts: value.reshape(-1, parts, half, value.shape[-1]).transpose(1, 0, 2, 3).reshape(-1, value.shape[-1]).T
    convolved = whole(arrived[:, :width], seqs)
    return (
        (gate.astype(jnp.float32) * convolved).astype(jnp.bfloat16),
        (upstream.astype(jnp.float32) * convolved).astype(jnp.bfloat16),
        whole(arrived[:, width : 2 * width], seqs).astype(jnp.bfloat16),
        whole(arrived[:, 2 * width :], 1),
    )


def shards(hyena_input, gate_input, filter_taps, cotangent):
    signal, gate, upstream = hyena_input[0], gate_input[0], cotangent[0]
    rows, channels = signal.shape
    blocks, seqs = lax.axis_size("context"), lax.axis_size("dp")
    owners = blocks * seqs
    half = channels // owners // seqs
    scale = 1.0 / math.sqrt(seqs * blocks * rows)
    if seqs == 2 and blocks in (2, 4, 8) and rows == LANES and channels % (2 * LANES) == 0 and channels // blocks in (16, 32, 64, 128, 256):
        outputs = tiled_shards(signal, gate, filter_taps, upstream, blocks, channels // blocks // 2, scale)
    else:
        leaving = pack_plain(signal, gate, filter_taps, upstream, seqs, half)
        arrived = lax.all_to_all(leaving, ("context", "dp"), 0, 0, tiled=True)
        leaving = core_plain(arrived, blocks, seqs, half, scale)
        arrived = lax.all_to_all(leaving, ("context", "dp"), 0, 0, tiled=True)
        outputs = unpack_plain(arrived, gate, upstream, seqs, half)
    gated, gate_grad, input_grad, filter_grad = outputs
    return gated[None], gate_grad[None], input_grad[None], filter_grad


def solution(mesh):
    placed = P(("groups", "dp"), "context", None)
    return jax.shard_map(
        shards,
        mesh=mesh,
        in_specs=(placed, placed, P("context", "groups"), placed),
        out_specs=(placed, placed, placed, P("context", ("groups", "dp"))),
        check_vma=False,
    )
```
